32 devices in a mesh: dom: 8 (over z, y), sub: 4 (over x, core).
Axes of the slice: x: 2, y: 2, z: 4, core: 2. Of those that a mesh axis runs over, the one named last changes fastest.
Arguments:
- history: bfloat16 [32768, 256], P(('dom', 'sub')), may hold values from -140 to 140
- tile_weight: bfloat16 [256, 64, 128, 128], P(('dom', 'sub')), may hold values from 0 to 1.75, as said below
- tile_source: int32 [256, 64], P(('dom', 'sub')), may hold values from 0 to 63
- tile_live: int32 [256], P(('dom', 'sub')), may hold values from 8 to 64, as said below
- send_list: int32 [32, 8, 4], P(('dom', 'sub')), may hold values from 0 to 7
- degree: int32 [32768], P(('dom', 'sub')), may hold values from 16 to 64
- labels: int32 [32768], P(('dom', 'sub')), may hold values from 0 to 171
- neigh_weight: bfloat16 [256, 172], replicated, may hold values from -0.375 to 0.375
- self_weight: bfloat16 [256, 172], replicated, may hold values from -0.375 to 0.375
Outputs:
- grad_history: float32 [32768, 256], P(('dom', 'sub'))
- neigh_grad: float32 [256, 172], replicated
- self_grad: float32 [256, 172], replicated
The draws below stay inside these ranges and needn't reach their ends.
Inputs may be any that keep to these rules, and one draw needn't show every extreme that they name: `tile_live`: every device owns a block with all 64 tiles live. `tile_weight`: nonzero entries lie within 0.25 and 1.75.
All inputs are finite; a program needn't handle non-finite values.
Results may differ from the reference program's by a relative error of at most 0.0055.
Values may be sent and summed in bfloat16 or wider, within the bound.
A program may use at most 192 MiB of HBM per device.

```python
import jax
import jax.numpy as jnp
from jax import lax

F = 256
C = 172
BLK = 128
NB_DEV = 8
TILES = 64
HALO_DEV = 32
NB_PART = 32
SLOTS = 4
SRC = 64
NODE_BLOCKS = 256
NODES = 32768
N_DOM = 8
N_SUB = 4


def draw_history(key, part):
    values = jax.random.truncated_normal(key, -4.0, 4.0, (NODES, F), jnp.float32)
    return values.astype(jnp.bfloat16)


def draw_tile_weight(key, part):
    keys = jax.random.split(key, 2)
    shape = (NODE_BLOCKS, TILES, BLK, BLK)
    present = jax.random.randint(keys[0], shape, 0, 16) == 0
    values = jax.random.uniform(keys[1], shape, jnp.float32, 0.5, 1.5)
    return jnp.where(present, values, 0.0).astype(jnp.bfloat16)


def draw_tile_live(key, part):
    keys = jax.random.split(key, 2)
    floor_live = max(TILES // 8, 1)
    owners = NODE_BLOCKS // NB_DEV
    lowest = jax.random.randint(keys[0], (owners, 1), floor_live, TILES // 2 + 1)
    counts = jax.random.randint(keys[1], (owners, NB_DEV), lowest, TILES + 1)
    counts = counts.at[:, 0].set(TILES)
    return counts.reshape(-1).astype(jnp.int32)


def touch_ends(array, stream_key, smallest, largest):
    longest = array.shape.index(max(array.shape))
    spots = []
    for shift in (0, 1):
        where = [jax.random.randint(jax.random.fold_in(stream_key, axis), (), 0, length) for axis, length in enumerate(array.shape)]
        where[longest] = (where[longest] + shift) % array.shape[longest]
        spots.append(tuple(where))
    return array.at[spots[0]].set(smallest).at[spots[1]].set(largest)


def centred(rng, dims, spread, limit, kind=jnp.bfloat16):
    array = jax.random.normal(rng, dims, jnp.float32) * spread
    return jnp.minimum(jnp.maximum(array, -limit), limit).astype(kind)


def setup_inputs(seed: int = 0) -> dict:
    arg_keys = jax.random.split(jax.random.key(seed), 10)
    history = draw_history(jax.random.fold_in(arg_keys[9], 71), 0)
    tile_weight = draw_tile_weight(jax.random.fold_in(arg_keys[9], 71), 0)
    tile_source = touch_ends(jax.random.randint(arg_keys[2], (NODE_BLOCKS, TILES), 0, NB_DEV * N_SUB + HALO_DEV), jax.random.fold_in(arg_keys[2], 1), 0, (NB_DEV * N_SUB + HALO_DEV) - 1).astype(jnp.int32)
    tile_live = draw_tile_live(jax.random.fold_in(arg_keys[9], 71), 0)
    send_list = touch_ends(jax.random.randint(arg_keys[4], (N_DOM * N_SUB, N_DOM, SLOTS), 0, NB_DEV), jax.random.fold_in(arg_keys[4], 1), 0, NB_DEV - 1).astype(jnp.int32)
    degree = touch_ends(jax.random.randint(arg_keys[5], (NODES,), 16, 65), jax.random.fold_in(arg_keys[5], 1), 16, 64).astype(jnp.int32)
    labels = touch_ends(jax.random.randint(arg_keys[6], (NODES,), 0, C), jax.random.fold_in(arg_keys[6], 1), 0, C - 1).astype(jnp.int32)
    neigh_weight = centred(arg_keys[7], (F, C), F ** -0.5, 0.375)
    self_weight = centred(arg_keys[8], (F, C), F ** -0.5, 0.375)
    return {"history": history, "tile_weight": tile_weight, "tile_source": tile_source, "tile_live": tile_live, "send_list": send_list, "degree": degree, "labels": labels, "neigh_weight": neigh_weight, "self_weight": self_weight}


def live_mask(live_count):
    return (jnp.arange(TILES, dtype=jnp.int32)[None, :] < live_count[:, None]).astype(jnp.float32)


def halo_index(device, send_list):
    dom_index = device // N_SUB
    sub_index = device % N_SUB
    senders = jnp.arange(N_DOM, dtype=jnp.int32) * N_SUB + sub_index
    return (senders[:, None] * NB_DEV + send_list[senders, dom_index, :]).astype(jnp.int32)


def reference(history, tile_weight, tile_source, tile_live, send_list, degree, labels, neigh_weight, self_weight):
    devices_all = N_DOM * N_SUB
    blocks = history.reshape(NODE_BLOCKS, BLK, F)
    tile_block = tile_weight.reshape(devices_all, NB_DEV, TILES, BLK, BLK)
    source_dev = tile_source.reshape(devices_all, NB_DEV, TILES)
    live_dev = tile_live.reshape(devices_all, NB_DEV)
    deg_float = degree.astype(jnp.float32)
    deg_dev = deg_float.reshape(devices_all, NB_DEV, BLK)
    device_ids = jnp.arange(devices_all, dtype=jnp.int32)

    def forward(record):
        device, tiles_here, source_here, live_here, deg_here = record
        dom_index = device // N_SUB
        part_blocks = lax.dynamic_slice_in_dim(blocks, (dom_index * NB_PART).astype(jnp.int32), NB_PART, 0)
        halo_blocks = blocks[halo_index(device, send_list).reshape(-1)]
        sources = jnp.concatenate([part_blocks, halo_blocks], axis=0)
        gathered = sources[source_here].astype(jnp.float32)
        weights = tiles_here.astype(jnp.float32) * live_mask(live_here)[:, :, None, None]
        summed = jnp.einsum('btij,btjf->bif', weights, gathered, precision=lax.Precision.HIGHEST)
        return (summed / deg_here[:, :, None]).astype(jnp.bfloat16)

    aggregate = lax.map(forward, (device_ids, tile_block, source_dev, live_dev, deg_dev)).reshape(NODES, F)
    logits = jnp.dot(aggregate, neigh_weight, preferred_element_type=jnp.float32) + jnp.dot(history, self_weight, preferred_element_type=jnp.float32)
    predicted = jax.nn.softmax(logits, axis=-1)
    onehot = (labels[:, None] == jnp.arange(C, dtype=jnp.int32)[None, :]).astype(jnp.float32)
    residual = predicted - onehot
    delta = residual.astype(jnp.bfloat16)
    norm_factor = float(NODES) ** -0.5
    neigh_grad = jnp.dot(aggregate.T, delta, preferred_element_type=jnp.float32) * norm_factor
    self_grad = jnp.dot(history.T, delta, preferred_element_type=jnp.float32) * norm_factor
    scaled = (residual / deg_float[:, None]).astype(jnp.bfloat16)
    scaled_dev = scaled.reshape(devices_all, NB_DEV, BLK, C)

    def backward(record):
        tiles_here, source_here, live_here, scaled_here = record
        weights = tiles_here.astype(jnp.float32) * live_mask(live_here)[:, :, None, None]
        per_tile = jnp.einsum('btij,bic->btjc', weights, scaled_here.astype(jnp.float32), precision=lax.Precision.HIGHEST)
        by_source = jax.ops.segment_sum(per_tile.reshape(NB_DEV * TILES, BLK, C), source_here.reshape(-1), num_segments=SRC)
        return by_source[:NB_PART].astype(jnp.bfloat16), by_source[NB_PART:]

    local_parts, halo_parts = lax.map(backward, (tile_block, source_dev, live_dev, scaled_dev))
    local_grad = local_parts.astype(jnp.float32).reshape(N_DOM, N_SUB, NB_PART, BLK, C).sum(axis=1).reshape(NODE_BLOCKS, BLK, C)
    targets = lax.map(lambda device: halo_index(device, send_list), device_ids).reshape(-1)
    boundary_grad = jax.ops.segment_sum(halo_parts.reshape(devices_all * HALO_DEV, BLK, C), targets, num_segments=NODE_BLOCKS)
    backward_sum = (local_grad + boundary_grad).reshape(NODES, C)
    grad_history = jnp.dot(backward_sum, neigh_weight.astype(jnp.float32).T, precision=lax.Precision.HIGHEST) + jnp.dot(delta, self_weight.T, preferred_element_type=jnp.float32)
    return (grad_history, neigh_grad, self_grad)
```

```python
import functools

import jax
import jax.numpy as jnp
from jax import lax
from jax.experimental import pallas as pl
from jax.experimental.pallas import tpu as pltpu
from jax.sharding import PartitionSpec as P

VMEM_BYTES = 58 * 1024 * 1024
CHUNK = 1024


def params():
    return pltpu.CompilerParams(vmem_limit_bytes=VMEM_BYTES)


def whole():
    return pl.BlockSpec(memory_space=pltpu.VMEM)


def comm_params(number):
    return pltpu.CompilerParams(
        vmem_limit_bytes=VMEM_BYTES, collective_id=number, has_side_effects=True
    )


def remote(src, dst, send, recv, axis, target):
    return pltpu.make_async_remote_copy(
        src_ref=src,
        dst_ref=dst,
        send_sem=send,
        recv_sem=recv,
        device_id={axis: target},
        device_id_type=pl.DeviceIdType.MESH,
    )


def greet(counts):
    barrier = pltpu.get_barrier_semaphore()
    for axis, count in counts:
        me = lax.axis_index(axis)
        for r in range(1, count):
            pl.semaphore_signal(
                barrier,
                inc=1,
                device_id={axis: lax.rem(me + r, count)},
                device_id_type=pl.DeviceIdType.MESH,
            )
    return barrier, sum(count - 1 for _, count in counts)


def send_kernel(
    doms, subs, slots, list_ref, own_ref, part_ref, halo_ref, outgoing, own_sems, *sems
):
    dom_send, dom_recv, sub_send, sub_recv = sems
    dom, sub = lax.axis_index("dom"), lax.axis_index("sub")
    barrier, count = greet((("dom", doms), ("sub", subs)))
    for n in range(doms * slots):
        outgoing[n // slots, n % slots] = own_ref[list_ref[n]]
    pl.semaphore_wait(barrier, count)
    copies = []
    for r in sorted(range(1, doms), key=lambda r: abs(r - doms // 2)):
        peer = lax.rem(dom + r, doms)
        copies.append(
            remote(
                outgoing.at[peer], halo_ref.at[dom], dom_send.at[r], dom_recv.at[r], "dom", peer
            )
        )
        copies[-1].start()
    for r in range(1, subs):
        peer = lax.rem(sub + r, subs)
        copies.append(
            remote(own_ref, part_ref.at[sub], sub_send.at[r], sub_recv.at[r], "sub", peer)
        )
        copies[-1].start()
    mine = (
        pltpu.make_async_copy(outgoing.at[dom], halo_ref.at[dom], own_sems.at[0]),
        pltpu.make_async_copy(own_ref, part_ref.at[sub], own_sems.at[1]),
    )
    for copy in mine:
        copy.start()
    for copy in mine:
        copy.wait()
    for copy in copies:
        copy.wait()


def send_history(own_blocks, flat_list, doms, subs, slots):
    block = own_blocks.shape[1:]
    dma = pltpu.SemaphoreType.DMA
    return pl.pallas_call(
        functools.partial(send_kernel, doms, subs, slots),
        out_shape=(
            jax.ShapeDtypeStruct((subs,) + own_blocks.shape, own_blocks.dtype),
            jax.ShapeDtypeStruct((doms, slots) + block, own_blocks.dtype),
        ),
        in_specs=[pl.BlockSpec(memory_space=pltpu.SMEM), whole()],
        out_specs=(pl.BlockSpec(memory_space=pl.ANY),) * 2,
        scratch_shapes=[
            pltpu.VMEM((doms, slots) + block, own_blocks.dtype),
            dma((2,)),
            dma((doms,)),
            dma((doms,)),
            dma((subs,)),
            dma((subs,)),
        ],
        compiler_params=comm_params(1),
        name="send_history",
    )(flat_list, own_blocks)


def return_kernel(
    doms,
    subs,
    slots,
    term_ref,
    grads_ref,
    local_ref,
    halo_ref,
    all_ref,
    quarters,
    quarter,
    pieces,
    joined,
    result,
    own_sems,
    *sems,
):
    (halo_send, halo_recv, local_send, local_recv) = sems[:4]
    (first_send, first_recv, second_send, second_recv) = sems[4:8]
    (third_send, third_recv, fourth_send, fourth_recv) = sems[8:]
    dom, sub = lax.axis_index("dom"), lax.axis_index("sub")
    blocks = local_ref.shape[1]
    part = subs * blocks
    barrier, count = greet((("dom", doms), ("sub", subs)))
    pl.semaphore_wait(barrier, count)

    def dom_peers():
        return [(r, lax.rem(dom + r, doms)) for r in range(1, doms)]

    def sub_peers():
        return [(r, lax.rem(sub + r, subs)) for r in range(1, subs)]

    def run(copies):
        for copy in copies:
            copy.start()
        return copies

    def finish_all(copies):
        for copy in copies:
            copy.wait()

    first = run(
        [
            remote(
                grads_ref.at[p], quarters.at[r], first_send.at[r], first_recv.at[r], "sub", p
            )
            for r, p in sub_peers()
        ]
    )
    big = run(
        [
            remote(
                term_ref.at[pl.ds(part + p * slots, slots)],
                halo_ref.at[pl.ds(dom * slots, slots)],
                halo_send.at[r],
                halo_recv.at[r],
                "dom",
                p,
            )
            for r, p in dom_peers()
        ]
        + [
            remote(
                term_ref.at[pl.ds(p * blocks, blocks)],
                local_ref.at[r],
                local_send.at[r],
                local_recv.at[r],
                "sub",
                p,
            )
            for r, p in sub_peers()
        ]
    )
    mine = run(
        [
            pltpu.make_async_copy(
                term_ref.at[pl.ds(part + dom * slots, slots)],
                halo_ref.at[pl.ds(dom * slots, slots)],
                own_sems.at[0],
            ),
            pltpu.make_async_copy(
                term_ref.at[pl.ds(sub * blocks, blocks)], local_ref.at[0], own_sems.at[1]
            ),
        ]
    )
    finish_all(first)
    total = grads_ref[sub]
    for r in range(1, subs):
        total += quarters[r]
    quarter[...] = total
    second = run(
        [
            remote(quarter.at[p], pieces.at[r], second_send.at[r], second_recv.at[r], "dom", p)
            for r, p in dom_peers()
        ]
    )
    finish_all(second)
    total = quarter[dom]
    for r in range(1, doms):
        total += pieces[r]
    joined[dom] = total
    third = run(
        [
            remote(
                joined.at[dom], joined.at[dom], third_send.at[r], third_recv.at[r], "dom", p
            )
            for r, p in dom_peers()
        ]
    )
    finish_all(third)
    result[sub] = joined[...]
    fourth = run(
        [
            remote(joined, result.at[sub], fourth_send.at[r], fourth_recv.at[r], "sub", p)
            for r, p in sub_peers()
        ]
    )
    finish_all(fourth)
    all_ref[...] = result[...]
    finish_all(mine)
    finish_all(big)


def return_terms(term, grads, doms, subs, slots, blocks):
    dma = pltpu.SemaphoreType.DMA
    block = term.shape[1:]
    piece = grads.shape[2:]
    counts = [doms, doms, subs, subs, subs, subs, doms, doms, doms, doms, subs, subs]
    return pl.pallas_call(
        functools.partial(return_kernel, doms, subs, slots),
        out_shape=(
            jax.ShapeDtypeStruct((subs, blocks) + block, term.dtype),
            jax.ShapeDtypeStruct((doms * slots,) + block, term.dtype),
            jax.ShapeDtypeStruct(grads.shape, grads.dtype),
        ),
        in_specs=[pl.BlockSpec(memory_space=pl.ANY), whole()],
        out_specs=(pl.BlockSpec(memory_space=pl.ANY),) * 2 + (whole(),),
        scratch_shapes=[
            pltpu.VMEM(grads.shape, grads.dtype),
            pltpu.VMEM((doms,) + piece, grads.dtype),
            pltpu.VMEM((doms,) + piece, grads.dtype),
            pltpu.VMEM((doms,) + piece, grads.dtype),
            pltpu.VMEM(grads.shape, grads.dtype),
            dma((2,)),
        ]
        + [dma((count,)) for count in counts],
        compiler_params=comm_params(2),
        name="return_terms",
    )(term, grads)


def dense_kernel(source_ref, live_ref, tile_ref, out_ref, total):
    block = pl.program_id(0)
    rows = tile_ref.shape[2]
    total[...] = jnp.zeros_like(total)

    def add(t, _):
        source = source_ref[block, t]
        total[source] += tile_ref[0, t].astype(jnp.float32)
        return 0

    lax.fori_loop(0, live_ref[block], add, 0)
    for source in range(total.shape[0]):
        out_ref[:, source * rows : (source + 1) * rows] = total[source].astype(out_ref.dtype)


def dense_adjacency(tile_source, tile_live, tile_weight, source_total):
    blocks, slots, rows, _ = tile_weight.shape
    return pl.pallas_call(
        dense_kernel,
        out_shape=jax.ShapeDtypeStruct((blocks * rows, source_total * rows), tile_weight.dtype),
        grid_spec=pltpu.PrefetchScalarGridSpec(
            num_scalar_prefetch=2,
            grid=(blocks,),
            in_specs=[pl.BlockSpec((1, slots, rows, rows), lambda b, *_: (b, 0, 0, 0))],
            out_specs=pl.BlockSpec((rows, source_total * rows), lambda b, *_: (b, 0)),
            scratch_shapes=[pltpu.VMEM((source_total, rows, rows), jnp.float32)],
        ),
        compiler_params=params(),
        cost_estimate=pl.CostEstimate(
            flops=4 * tile_weight.size, bytes_accessed=4 * tile_weight.size, transcendentals=0
        ),
        name="dense",
    )(tile_source, tile_live, tile_weight)


def layer_kernel(
    classes,
    dense_hbm,
    part_ref,
    halo_ref,
    history_ref,
    degree_ref,
    label_ref,
    neigh_ref,
    self_ref,
    term_ref,
    delta_ref,
    grads_ref,
    dense,
    total,
    scaled_t,
    sems,
):
    columns = dense.shape[1]
    chunks = columns // CHUNK
    part_rows = part_ref.shape[0]

    def fetch(c):
        return pltpu.make_async_copy(
            dense_hbm.at[:, pl.ds(c * CHUNK, CHUNK)], dense.at[:, pl.ds(c * CHUNK, CHUNK)], sems.at[c]
        )

    for c in range(chunks):
        fetch(c).start()
    for c in range(chunks):
        fetch(c).wait()
        start = c * CHUNK
        if start < part_rows:
            sources = part_ref[start : start + CHUNK, :]
        else:
            sources = halo_ref[start - part_rows : start - part_rows + CHUNK, :]
        product = jnp.dot(
            dense[:, start : start + CHUNK], sources, preferred_element_type=jnp.float32
        )
        if c == 0:
            total[...] = product
        else:
            total[...] += product
    degree = degree_ref[...].astype(jnp.float32)
    aggregate = (total[...] / degree).astype(jnp.bfloat16)
    history = history_ref[...]
    logits = jnp.dot(aggregate, neigh_ref[...], preferred_element_type=jnp.float32) + jnp.dot(
        history, self_ref[...], preferred_element_type=jnp.float32
    )
    column = lax.broadcasted_iota(jnp.int32, logits.shape, 1)
    logits = jnp.where(column < classes, logits, -jnp.inf)
    exps = jnp.exp(logits - jnp.max(logits, axis=1, keepdims=True))
    predicted = exps / jnp.sum(exps, axis=1, keepdims=True)
    residual = predicted - (column == label_ref[...]).astype(jnp.float32)
    delta_ref[...] = residual.astype(jnp.bfloat16)
    scaled_t[...] = jnp.transpose(residual / degree)[: scaled_t.shape[0]].astype(jnp.bfloat16)
    delta_t = jnp.transpose(residual).astype(jnp.bfloat16)
    width = neigh_ref.shape[1]
    grads_ref[:width, :] = jnp.dot(delta_t, aggregate, preferred_element_type=jnp.float32)
    grads_ref[width:, :] = jnp.dot(delta_t, history, preferred_element_type=jnp.float32)
    rows = term_ref.shape[2]
    step = 4 * rows
    for start in range(0, columns, step):
        term = jnp.dot(
            scaled_t[...], dense[:, start : start + step], preferred_element_type=jnp.float32
        ).astype(jnp.bfloat16)
        for i in range(4):
            term_ref[start // rows + i] = term[:, i * rows : (i + 1) * rows]


def layer(dense, part, halo, history, degree, labels, neigh, self_w, classes, rows):
    nodes, columns = dense.shape
    width = history.shape[1]
    padded = neigh.shape[1]
    short = -(-classes // 16) * 16
    return pl.pallas_call(
        functools.partial(layer_kernel, classes),
        out_shape=(
            jax.ShapeDtypeStruct((columns // rows, short, rows), jnp.bfloat16),
            jax.ShapeDtypeStruct((nodes, padded), jnp.bfloat16),
            jax.ShapeDtypeStruct((2 * padded, width), jnp.float32),
        ),
        in_specs=[pl.BlockSpec(memory_space=pl.ANY)] + [whole()] * 7,
        out_specs=(whole(),) * 3,
        scratch_shapes=[
            pltpu.VMEM((nodes, columns), jnp.bfloat16),
            pltpu.VMEM((nodes, width), jnp.float32),
            pltpu.VMEM((short, nodes), jnp.bfloat16),
            pltpu.SemaphoreType.DMA((columns // CHUNK,)),
        ],
        compiler_params=params(),
        cost_estimate=pl.CostEstimate(
            flops=4 * nodes * columns * width, bytes_accessed=2 * dense.size, transcendentals=0
        ),
        name="layer",
    )(dense, part, halo, history, degree, labels, neigh, self_w)


def finish_kernel(list_ref, local_ref, halo_ref, delta_ref, neigh_ref, self_ref, out_ref, total):
    blocks, short, rows = total.shape
    for i in range(blocks):
        value = local_ref[0, i].astype(jnp.float32)
        for s in range(1, local_ref.shape[0]):
            value += local_ref[s, i].astype(jnp.float32)
        total[i] = value

    def add(n, _):
        total[list_ref[n]] += halo_ref[n].astype(jnp.float32)
        return 0

    lax.fori_loop(0, halo_ref.shape[0], add, 0)
    neigh = neigh_ref[...]
    for i in range(blocks):
        value = total[i]
        value = jnp.transpose(
            jnp.concatenate([value, jnp.zeros((neigh.shape[1] - short, rows), jnp.float32)], axis=0)
        )
        high = value.astype(jnp.bfloat16)
        low = (value - high.astype(jnp.float32)).astype(jnp.bfloat16)
        dims = (((1,), (1,)), ((), ()))
        out = lax.dot_general(high, neigh, dims, preferred_element_type=jnp.float32)
        out += lax.dot_general(low, neigh, dims, preferred_element_type=jnp.float32)
        out += lax.dot_general(
            delta_ref[i * rows : (i + 1) * rows, :],
            self_ref[...],
            dims,
            preferred_element_type=jnp.float32,
        )
        out_ref[i * rows : (i + 1) * rows, :] = out


def finish(flat_list, local, halo, delta, neigh, self_w):
    blocks, short, rows = local.shape[1:]
    return pl.pallas_call(
        finish_kernel,
        out_shape=jax.ShapeDtypeStruct((delta.shape[0], neigh.shape[0]), jnp.float32),
        in_specs=[pl.BlockSpec(memory_space=pltpu.SMEM)] + [whole()] * 5,
        out_specs=whole(),
        scratch_shapes=[pltpu.VMEM((blocks, short, rows), jnp.float32)],
        compiler_params=params(),
        name="finish",
    )(flat_list, local, halo, delta, neigh, self_w)


def per_device(
    history,
    tile_weight,
    tile_source,
    tile_live,
    send_list,
    degree,
    labels,
    neigh_weight,
    self_weight,
):
    block_count, _, rows, _ = tile_weight.shape
    width = history.shape[1]
    classes = neigh_weight.shape[1]
    dom_count, sub_count = lax.axis_size("dom"), lax.axis_size("sub")
    devices = dom_count * sub_count
    slots = send_list.shape[2]
    part_blocks = block_count * sub_count
    source_total = part_blocks + dom_count * slots
    nodes_all = history.shape[0] * devices
    flat_list = send_list.reshape(-1)
    own_blocks = history.reshape(block_count, rows, width)
    part, halo = send_history(own_blocks, flat_list, dom_count, sub_count, slots)
    dense = dense_adjacency(tile_source, tile_live, tile_weight, source_total)
    pad = ((0, 0), (0, -classes % 128))
    neigh = jnp.pad(neigh_weight, pad)
    self_w = jnp.pad(self_weight, pad)
    padded = neigh.shape[1]
    term, delta, grads = layer(
        dense,
        part.reshape(-1, width),
        halo.reshape(-1, width),
        history,
        degree[:, None],
        labels[:, None],
        neigh,
        self_w,
        classes,
        rows,
    )
    pieces = (sub_count, dom_count, 2 * padded // devices, width)
    local_back, halo_back, grads_all = return_terms(
        term, grads.reshape(pieces), dom_count, sub_count, slots, block_count
    )
    grads_all = grads_all.reshape(2, padded, width)[:, :classes].transpose(0, 2, 1)
    grads_all = grads_all * float(nodes_all) ** (-0.5)
    grad_history = finish(
        flat_list,
        local_back,
        halo_back,
        delta,
        neigh,
        self_w,
    )
    return (grad_history, grads_all[0], grads_all[1])


def solution(mesh):
    placed = (
        P(("dom", "sub"), None),
        P(("dom", "sub"), None, None, None),
        P(("dom", "sub"), None),
        P(("dom", "sub")),
        P(("dom", "sub"), None, None),
        P(("dom", "sub")),
        P(("dom", "sub")),
        P(),
        P(),
    )
    return jax.shard_map(
        per_device,
        mesh=mesh,
        in_specs=placed,
        out_specs=(P(("dom", "sub"), None), P(), P()),
        check_vma=False,
    )
```

```python
import functools

import jax
import jax.numpy as jnp
from jax import lax
from jax.experimental import pallas as pl
from jax.experimental.pallas import tpu as pltpu
from jax.sharding import PartitionSpec as P

VMEM_BYTES = 58 * 1024 * 1024
CHUNK = 1024


def params():
    return pltpu.CompilerParams(vmem_limit_bytes=VMEM_BYTES)


def whole():
    return pl.BlockSpec(memory_space=pltpu.VMEM)


def comm_params(number):
    return pltpu.CompilerParams(
        vmem_limit_bytes=VMEM_BYTES, collective_id=number, has_side_effects=True
    )


def remote(src, dst, send, recv, axis, target):
    return pltpu.make_async_remote_copy(
        src_ref=src,
        dst_ref=dst,
        send_sem=send,
        recv_sem=recv,
        device_id={axis: target},
        device_id_type=pl.DeviceIdType.MESH,
    )


def greet(counts):
    barrier = pltpu.get_barrier_semaphore()
    for axis, count in counts:
        me = lax.axis_index(axis)
        for r in range(1, count):
            pl.semaphore_signal(
                barrier,
                inc=1,
                device_id={axis: lax.rem(me + r, count)},
                device_id_type=pl.DeviceIdType.MESH,
            )
    return barrier, sum(count - 1 for _, count in counts)


def send_kernel(
    doms, subs, slots, list_ref, own_ref, part_ref, halo_ref, outgoing, own_sems, *sems
):
    dom_send, dom_recv, sub_send, sub_recv = sems
    dom, sub = lax.axis_index("dom"), lax.axis_index("sub")
    barrier, count = greet((("dom", doms), ("sub", subs)))
    for n in range(doms * slots):
        outgoing[n // slots, n % slots] = own_ref[list_ref[n]]
    pl.semaphore_wait(barrier, count)
    copies = []
    for r in sorted(range(1, doms), key=lambda r: abs(r - doms // 2)):
        peer = lax.rem(dom + r, doms)
        copies.append(
            remote(
                outgoing.at[peer], halo_ref.at[dom], dom_send.at[r], dom_recv.at[r], "dom", peer
            )
        )
        copies[-1].start()
    for r in range(1, subs):
        peer = lax.rem(sub + r, subs)
        copies.append(
            remote(own_ref, part_ref.at[sub], sub_send.at[r], sub_recv.at[r], "sub", peer)
        )
        copies[-1].start()
    mine = (
        pltpu.make_async_copy(outgoing.at[dom], halo_ref.at[dom], own_sems.at[0]),
        pltpu.make_async_copy(own_ref, part_ref.at[sub], own_sems.at[1]),
    )
    for copy in mine:
        copy.start()
    for copy in mine:
        copy.wait()
    for copy in copies:
        copy.wait()


def send_history(own_blocks, flat_list, doms, subs, slots):
    block = own_blocks.shape[1:]
    dma = pltpu.SemaphoreType.DMA
    return pl.pallas_call(
        functools.partial(send_kernel, doms, subs, slots),
        out_shape=(
            jax.ShapeDtypeStruct((subs,) + own_blocks.shape, own_blocks.dtype),
            jax.ShapeDtypeStruct((doms, slots) + block, own_blocks.dtype),
        ),
        in_specs=[pl.BlockSpec(memory_space=pltpu.SMEM), whole()],
        out_specs=(pl.BlockSpec(memory_space=pl.ANY),) * 2,
        scratch_shapes=[
            pltpu.VMEM((doms, slots) + block, own_blocks.dtype),
            dma((2,)),
            dma((doms,)),
            dma((doms,)),
            dma((subs,)),
            dma((subs,)),
        ],
        compiler_params=comm_params(1),
        name="send_history",
    )(flat_list, own_blocks)


def return_kernel(
    doms,
    subs,
    slots,
    term_ref,
    grads_ref,
    local_ref,
    halo_ref,
    all_ref,
    quarters,
    quarter,
    pieces,
    joined,
    result,
    own_sems,
    *sems,
):
    (halo_send, halo_recv, local_send, local_recv) = sems[:4]
    (first_send, first_recv, second_send, second_recv) = sems[4:8]
    (third_send, third_recv, fourth_send, fourth_recv) = sems[8:]
    dom, sub = lax.axis_index("dom"), lax.axis_index("sub")
    blocks = local_ref.shape[1]
    part = subs * blocks
    barrier, count = greet((("dom", doms), ("sub", subs)))
    pl.semaphore_wait(barrier, count)

    def dom_peers():
        return [(r, lax.rem(dom + r, doms)) for r in range(1, doms)]

    def sub_peers():
        return [(r, lax.rem(sub + r, subs)) for r in range(1, subs)]

    def run(copies):
        for copy in copies:
            copy.start()
        return copies

    def finish_all(copies):
        for copy in copies:
            copy.wait()

    first = run(
        [
            remote(
                grads_ref.at[p], quarters.at[r], first_send.at[r], first_recv.at[r], "sub", p
            )
            for r, p in sub_peers()
        ]
    )
    big = run(
        [
            remote(
                term_ref.at[pl.ds(part + p * slots, slots)],
                halo_ref.at[pl.ds(dom * slots, slots)],
                halo_send.at[r],
                halo_recv.at[r],
                "dom",
                p,
            )
            for r, p in dom_peers()
        ]
        + [
            remote(
                term_ref.at[pl.ds(p * blocks, blocks)],
                local_ref.at[r],
                local_send.at[r],
                local_recv.at[r],
                "sub",
                p,
            )
            for r, p in sub_peers()
        ]
    )
    mine = run(
        [
            pltpu.make_async_copy(
                term_ref.at[pl.ds(part + dom * slots, slots)],
                halo_ref.at[pl.ds(dom * slots, slots)],
                own_sems.at[0],
            ),
            pltpu.make_async_copy(
                term_ref.at[pl.ds(sub * blocks, blocks)], local_ref.at[0], own_sems.at[1]
            ),
        ]
    )
    finish_all(first)
    total = grads_ref[sub]
    for r in range(1, subs):
        total += quarters[r]
    quarter[...] = total
    second = run(
        [
            remote(quarter.at[p], pieces.at[r], second_send.at[r], second_recv.at[r], "dom", p)
            for r, p in dom_peers()
        ]
    )
    finish_all(second)
    total = quarter[dom]
    for r in range(1, doms):
        total += pieces[r]
    joined[dom] = total
    third = run(
        [
            remote(
                joined.at[dom], joined.at[dom], third_send.at[r], third_recv.at[r], "dom", p
            )
            for r, p in dom_peers()
        ]
    )
    finish_all(third)
    result[sub] = joined[...]
    fourth = run(
        [
            remote(joined, result.at[sub], fourth_send.at[r], fourth_recv.at[r], "sub", p)
            for r, p in sub_peers()
        ]
    )
    finish_all(fourth)
    all_ref[...] = result[...]
    finish_all(mine)
    finish_all(big)


def return_terms(term, grads, doms, subs, slots, blocks):
    dma = pltpu.SemaphoreType.DMA
    block = term.shape[1:]
    piece = grads.shape[2:]
    counts = [doms, doms, subs, subs, subs, subs, doms, doms, doms, doms, subs, subs]
    return pl.pallas_call(
        functools.partial(return_kernel, doms, subs, slots),
        out_shape=(
            jax.ShapeDtypeStruct((subs, blocks) + block, term.dtype),
            jax.ShapeDtypeStruct((doms * slots,) + block, term.dtype),
            jax.ShapeDtypeStruct(grads.shape, grads.dtype),
        ),
        in_specs=[pl.BlockSpec(memory_space=pl.ANY), whole()],
        out_specs=(pl.BlockSpec(memory_space=pl.ANY),) * 2 + (whole(),),
        scratch_shapes=[
            pltpu.VMEM(grads.shape, grads.dtype),
            pltpu.VMEM((doms,) + piece, grads.dtype),
            pltpu.VMEM((doms,) + piece, grads.dtype),
            pltpu.VMEM((doms,) + piece, grads.dtype),
            pltpu.VMEM(grads.shape, grads.dtype),
            dma((2,)),
        ]
        + [dma((count,)) for count in counts],
        compiler_params=comm_params(2),
        name="return_terms",
    )(term, grads)


def dense_kernel(source_ref, live_ref, tile_ref, out_ref, total):
    block = pl.program_id(0)
    rows = tile_ref.shape[2]
    total[...] = jnp.zeros_like(total)

    def add(t, _):
        source = source_ref[block, t]
        total[source] += tile_ref[0, t].astype(jnp.float32)
        return 0

    lax.fori_loop(0, live_ref[block], add, 0)
    for source in range(total.shape[0]):
        out_ref[:, source * rows : (source + 1) * rows] = total[source].astype(out_ref.dtype)


def dense_adjacency(tile_source, tile_live, tile_weight, source_total):
    blocks, slots, rows, _ = tile_weight.shape
    return pl.pallas_call(
        dense_kernel,
        out_shape=jax.ShapeDtypeStruct((blocks * rows, source_total * rows), tile_weight.dtype),
        grid_spec=pltpu.PrefetchScalarGridSpec(
            num_scalar_prefetch=2,
            grid=(blocks,),
            in_specs=[pl.BlockSpec((1, slots, rows, rows), lambda b, *_: (b, 0, 0, 0))],
            out_specs=pl.BlockSpec((rows, source_total * rows), lambda b, *_: (b, 0)),
            scratch_shapes=[pltpu.VMEM((source_total, rows, rows), jnp.float32)],
        ),
        compiler_params=params(),
        cost_estimate=pl.CostEstimate(
            flops=4 * tile_weight.size, bytes_accessed=4 * tile_weight.size, transcendentals=0
        ),
        name="dense",
    )(tile_source, tile_live, tile_weight)


def as_column(ref):
    rows = ref.shape[1]
    parts = [
        jnp.transpose(jnp.broadcast_to(ref[i : i + 1, :].astype(jnp.float32), (rows, rows)))
        for i in range(ref.shape[0])
    ]
    return jnp.concatenate(parts, axis=0)[:, :1]


def layer_kernel(
    classes,
    dense_hbm,
    part_ref,
    halo_ref,
    history_ref,
    degree_ref,
    label_ref,
    neigh_ref,
    self_ref,
    term_ref,
    delta_ref,
    grads_ref,
    dense,
    total,
    scaled_t,
    sems,
):
    columns = dense.shape[1]
    chunks = columns // CHUNK
    part_rows = part_ref.shape[0]

    def fetch(c):
        return pltpu.make_async_copy(
            dense_hbm.at[:, pl.ds(c * CHUNK, CHUNK)], dense.at[:, pl.ds(c * CHUNK, CHUNK)], sems.at[c]
        )

    for c in range(chunks):
        fetch(c).start()
    for c in range(chunks):
        fetch(c).wait()
        start = c * CHUNK
        if start < part_rows:
            sources = part_ref[start : start + CHUNK, :]
        else:
            sources = halo_ref[start - part_rows : start - part_rows + CHUNK, :]
        product = jnp.dot(
            dense[:, start : start + CHUNK], sources, preferred_element_type=jnp.float32
        )
        if c == 0:
            total[...] = product
        else:
            total[...] += product
    degree = as_column(degree_ref)
    aggregate = (total[...] / degree).astype(jnp.bfloat16)
    history = history_ref[...]
    logits = jnp.dot(aggregate, neigh_ref[...], preferred_element_type=jnp.float32) + jnp.dot(
        history, self_ref[...], preferred_element_type=jnp.float32
    )
    column = lax.broadcasted_iota(jnp.int32, logits.shape, 1)
    logits = jnp.where(column < classes, logits, -jnp.inf)
    exps = jnp.exp(logits - jnp.max(logits, axis=1, keepdims=True))
    predicted = exps / jnp.sum(exps, axis=1, keepdims=True)
    residual = predicted - (column == as_column(label_ref).astype(jnp.int32)).astype(jnp.float32)
    delta_ref[...] = residual.astype(jnp.bfloat16)
    scaled_t[...] = jnp.transpose(residual / degree)[: scaled_t.shape[0]].astype(jnp.bfloat16)
    delta_t = jnp.transpose(residual).astype(jnp.bfloat16)
    width = neigh_ref.shape[1]
    grads_ref[:width, :] = jnp.dot(delta_t, aggregate, preferred_element_type=jnp.float32)
    grads_ref[width:, :] = jnp.dot(delta_t, history, preferred_element_type=jnp.float32)
    rows = term_ref.shape[2]
    step = 8 * rows
    for start in range(0, columns, step):
        term = jnp.dot(
            scaled_t[...], dense[:, start : start + step], preferred_element_type=jnp.float32
        ).astype(jnp.bfloat16)
        for i in range(8):
            term_ref[start // rows + i] = term[:, i * rows : (i + 1) * rows]


def layer(dense, part, halo, history, degree, labels, neigh, self_w, classes, rows):
    nodes, columns = dense.shape
    width = history.shape[1]
    padded = neigh.shape[1]
    short = -(-classes // 16) * 16
    return pl.pallas_call(
        functools.partial(layer_kernel, classes),
        out_shape=(
            jax.ShapeDtypeStruct((columns // rows, short, rows), jnp.bfloat16),
            jax.ShapeDtypeStruct((nodes, padded), jnp.bfloat16),
            jax.ShapeDtypeStruct((2 * padded, width), jnp.float32),
        ),
        in_specs=[pl.BlockSpec(memory_space=pl.ANY)] + [whole()] * 7,
        out_specs=(whole(),) * 3,
        scratch_shapes=[
            pltpu.VMEM((nodes, columns), jnp.bfloat16),
            pltpu.VMEM((nodes, width), jnp.float32),
            pltpu.VMEM((short, nodes), jnp.bfloat16),
            pltpu.SemaphoreType.DMA((columns // CHUNK,)),
        ],
        compiler_params=params(),
        cost_estimate=pl.CostEstimate(
            flops=4 * nodes * columns * width, bytes_accessed=2 * dense.size, transcendentals=0
        ),
        name="layer",
    )(dense, part, halo, history, degree, labels, neigh, self_w)


def finish_kernel(list_ref, local_ref, halo_ref, delta_ref, neigh_ref, self_ref, out_ref, total):
    blocks, short, rows = total.shape
    for i in range(blocks):
        value = local_ref[0, i].astype(jnp.float32)
        for s in range(1, local_ref.shape[0]):
            value += local_ref[s, i].astype(jnp.float32)
        total[i] = value

    def add(n, _):
        total[list_ref[n]] += halo_ref[n].astype(jnp.float32)
        return 0

    lax.fori_loop(0, halo_ref.shape[0], add, 0)
    neigh = neigh_ref[...]
    for i in range(blocks):
        value = total[i]
        value = jnp.transpose(
            jnp.concatenate([value, jnp.zeros((neigh.shape[1] - short, rows), jnp.float32)], axis=0)
        )
        high = value.astype(jnp.bfloat16)
        low = (value - high.astype(jnp.float32)).astype(jnp.bfloat16)
        dims = (((1,), (1,)), ((), ()))
        out = lax.dot_general(high, neigh, dims, preferred_element_type=jnp.float32)
        out += lax.dot_general(low, neigh, dims, preferred_element_type=jnp.float32)
        out += lax.dot_general(
            delta_ref[i * rows : (i + 1) * rows, :],
            self_ref[...],
            dims,
            preferred_element_type=jnp.float32,
        )
        out_ref[i * rows : (i + 1) * rows, :] = out


def finish(flat_list, local, halo, delta, neigh, self_w):
    blocks, short, rows = local.shape[1:]
    return pl.pallas_call(
        finish_kernel,
        out_shape=jax.ShapeDtypeStruct((delta.shape[0], neigh.shape[0]), jnp.float32),
        in_specs=[pl.BlockSpec(memory_space=pltpu.SMEM)] + [whole()] * 5,
        out_specs=whole(),
        scratch_shapes=[pltpu.VMEM((blocks, short, rows), jnp.float32)],
        compiler_params=params(),
        name="finish",
    )(flat_list, local, halo, delta, neigh, self_w)


def per_device(
    history,
    tile_weight,
    tile_source,
    tile_live,
    send_list,
    degree,
    labels,
    neigh_weight,
    self_weight,
):
    block_count, _, rows, _ = tile_weight.shape
    width = history.shape[1]
    classes = neigh_weight.shape[1]
    dom_count, sub_count = lax.axis_size("dom"), lax.axis_size("sub")
    devices = dom_count * sub_count
    slots = send_list.shape[2]
    part_blocks = block_count * sub_count
    source_total = part_blocks + dom_count * slots
    nodes_all = history.shape[0] * devices
    flat_list = send_list.reshape(-1)
    own_blocks = history.reshape(block_count, rows, width)
    part, halo = send_history(own_blocks, flat_list, dom_count, sub_count, slots)
    dense = dense_adjacency(tile_source, tile_live, tile_weight, source_total)
    pad = ((0, 0), (0, -classes % 128))
    neigh = jnp.pad(neigh_weight, pad)
    self_w = jnp.pad(self_weight, pad)
    padded = neigh.shape[1]
    term, delta, grads = layer(
        dense,
        part.reshape(-1, width),
        halo.reshape(-1, width),
        history,
        degree.reshape(block_count, rows),
        labels.reshape(block_count, rows),
        neigh,
        self_w,
        classes,
        rows,
    )
    pieces = (sub_count, dom_count, 2 * padded // devices, width)
    local_back, halo_back, grads_all = return_terms(
        term, grads.reshape(pieces), dom_count, sub_count, slots, block_count
    )
    grads_all = grads_all.reshape(2, padded, width)[:, :classes].transpose(0, 2, 1)
    grads_all = grads_all * float(nodes_all) ** (-0.5)
    grad_history = finish(
        flat_list,
        local_back,
        halo_back,
        delta,
        neigh,
        self_w,
    )
    return (grad_history, grads_all[0], grads_all[1])


def solution(mesh):
    placed = (
        P(("dom", "sub"), None),
        P(("dom", "sub"), None, None, None),
        P(("dom", "sub"), None),
        P(("dom", "sub")),
        P(("dom", "sub"), None, None),
        P(("dom", "sub")),
        P(("dom", "sub")),
        P(),
        P(),
    )
    return jax.shard_map(
        per_device,
        mesh=mesh,
        in_specs=placed,
        out_specs=(P(("dom", "sub"), None), P(), P()),
        check_vma=False,
    )
```
